32 devices in a mesh: dp: 8 (over y, x, core), tensor: 4 (over z).
Axes of the slice: x: 2, y: 2, z: 4, core: 2. Of those that a mesh axis runs over, the one named last changes fastest.
Arguments:
- width_side: bfloat16 [8, 1024, 1024], P(None, 'dp'), may hold values from -6 to 6
- hidden_side: bfloat16 [8, 1024, 12288], P(None, 'dp', 'tensor'), may hold values from -0.1875 to 0.1875
- block_owner: int32 [8], replicated, may hold values from 0 to 7, as said below
- basis_hidden: bfloat16 [8, 2, 12288, 3072], P('dp', None, 'tensor'), may hold values from -0.109375 to 0.109375
- basis_width: bfloat16 [8, 2, 1024, 1024], P('dp', None, 'tensor'), may hold values from -0.1875 to 0.1875
- values_hidden: bfloat16 [8, 2, 12288], P('dp', None, 'tensor'), may hold values from 0.29882812 to 3
- values_width: bfloat16 [8, 2, 1024], P('dp'), may hold values from 0.29882812 to 3
Outputs:
- preconditioned: bfloat16 [8, 12288, 1024], P(None, ('tensor', 'dp'))
The draws below stay inside these ranges and needn't reach their ends.
Inputs may be any that keep to these rules, and one draw needn't show every extreme that they name: `block_owner`: no owner holds more than 2 blocks, and some owner holds exactly 2.
All inputs are finite; a program needn't handle non-finite values.
Results may differ from the reference program's by a relative error of at most 0.023.
Values may be sent and summed in bfloat16 or wider, within the bound.
No kernel may reach another device: no remote copies, remote signals or barrier semaphores. Data moves between devices by JAX's collectives and lax.ppermute only.
A program may use at most 256 MiB of HBM per device.

```python
import math
import jax
import jax.numpy as jnp
from jax import lax

BW = 1024
FF = 12288
CAP = 2
TOK_DEV = 128
NBLK = 8
TOKENS = 1024
N_DP = 8
N_TENSOR = 4


def draw_block_owner(key, part):
    key = jax.random.fold_in(key, 11)
    first_key, second_key = jax.random.split(key, 2)
    owner_order = jax.random.permutation(first_key, N_DP).astype(jnp.int32)
    block_order = jax.random.permutation(second_key, NBLK).astype(jnp.int32)
    doubled = max(1, NBLK // 4)
    positions = jnp.arange(NBLK, dtype=jnp.int32)
    owner_slot = jnp.where(positions < 2 * doubled, positions // 2, positions - doubled).astype(jnp.int32)
    owners = owner_order[owner_slot]
    return owners[block_order].astype(jnp.int32)


def block_scale(own_key, shape, cuts, smallest, largest):
    factor_of = 1.0
    for position, parts in cuts:
        steps = jax.random.uniform(jax.random.fold_in(jax.random.fold_in(own_key, 6), position), (parts,), jnp.float32, smallest / len(cuts), largest / len(cuts))
        factor_of = factor_of * jnp.repeat(jnp.exp(steps), shape[position] // parts).reshape((-1,) + (1,) * (len(shape) - 1 - position))
    return factor_of


def centred(key, extent, scale, limit, pieces=(), held_as=jnp.bfloat16):
    entries = scale * jax.random.normal(key, extent, jnp.float32)
    if pieces:
        entries = entries * block_scale(key, extent, pieces, -0.22, 0.18)
    return jnp.clip(entries, -limit, limit).astype(held_as)


def setup_inputs(seed: int = 0) -> dict:
    seeds = jax.random.split(jax.random.key(seed), 8)
    width_side = centred(seeds[0], (NBLK, TOKENS, BW), 1.0, 6.0, ((1, 8),))
    hidden_side = centred(seeds[1], (NBLK, TOKENS, FF), TOKENS ** -0.5, 0.1875, ((1, 8), (2, 4)))
    block_owner = draw_block_owner(jax.random.fold_in(seeds[7], 71), 0)
    basis_hidden = centred(seeds[3], (N_DP, CAP, FF, FF // N_TENSOR), (FF // N_TENSOR) ** -0.5, 0.109375, ((0, 8), (2, 4)))
    basis_width = centred(seeds[4], (N_DP, CAP, BW, BW), BW ** -0.5, 0.1875, ((0, 8), (2, 4)))
    values_hidden = jnp.clip(jnp.exp(math.log(3.0) - 2.306499 * jax.random.uniform(seeds[5], (N_DP, CAP, FF), jnp.float32) ** block_scale(seeds[5], (N_DP, CAP, FF), ((0, 8), (2, 4)), -0.2, 0.2)), 0.29882812, 3.0).astype(jnp.bfloat16)
    values_width = jnp.clip(jnp.exp(math.log(3.0) - 2.306499 * jax.random.uniform(seeds[6], (N_DP, CAP, BW), jnp.float32) ** block_scale(seeds[6], (N_DP, CAP, BW), ((0, 8),), -0.2, 0.2)), 0.29882812, 3.0).astype(jnp.bfloat16)
    return dict(width_side=width_side, hidden_side=hidden_side, block_owner=block_owner, basis_hidden=basis_hidden, basis_width=basis_width, values_hidden=values_hidden, values_width=values_width)


damping_term = 0.1


def slot_ranks(block_owner):
    count_blocks = block_owner.shape[0]
    positions = jnp.arange(count_blocks, dtype=jnp.int32)
    earlier = positions[None, :] < positions[:, None]
    same_owner = block_owner[:, None] == block_owner[None, :]
    return jnp.sum(jnp.logical_and(earlier, same_owner).astype(jnp.int32), axis=1).astype(jnp.int32)


def to_wide(value):
    return lax.optimization_barrier(value.astype(jnp.bfloat16)).astype(jnp.float32)


def summed_gradient(width_rows, hidden_rows):
    def add_replica(replica, total):
        start = (replica * TOK_DEV).astype(jnp.int32)
        hidden_part = lax.dynamic_slice_in_dim(hidden_rows, start, TOK_DEV, 0).astype(jnp.float32)
        width_part = lax.dynamic_slice_in_dim(width_rows, start, TOK_DEV, 0).astype(jnp.float32)
        partial_grad = jnp.dot(hidden_part.T, width_part, precision=lax.Precision.HIGHEST)
        return total + to_wide(partial_grad)

    return lax.fori_loop(0, N_DP, add_replica, jnp.zeros((FF, BW), jnp.float32))


def reference(width_side, hidden_side, block_owner, basis_hidden, basis_width, values_hidden, values_width):
    ranks = slot_ranks(block_owner)
    part_rows = FF // N_TENSOR
    outputs = []
    for block_index in range(NBLK):
        gradient = to_wide(summed_gradient(width_side[block_index], hidden_side[block_index]))
        gradient = gradient.reshape(N_TENSOR, part_rows, BW)
        owner_now = block_owner[block_index]
        slot_now = ranks[block_index]
        hidden_basis = basis_hidden[owner_now, slot_now].astype(jnp.float32).reshape(N_TENSOR, part_rows, part_rows)
        width_basis = basis_width[owner_now, slot_now].astype(jnp.float32)
        hidden_values = values_hidden[owner_now, slot_now].astype(jnp.float32).reshape(N_TENSOR, part_rows)
        width_values = values_width[owner_now, slot_now].astype(jnp.float32)
        left = to_wide(jnp.einsum("tfi,tfw->tiw", hidden_basis, gradient, precision=lax.Precision.HIGHEST))
        middle = jnp.einsum("tiw,wv->tiv", left, width_basis, precision=lax.Precision.HIGHEST)
        scaled = to_wide(middle / (hidden_values[:, :, None] * width_values[None, None, :] + damping_term))
        turned = to_wide(jnp.einsum("tfi,tiv->tfv", hidden_basis, scaled, precision=lax.Precision.HIGHEST))
        final = jnp.einsum("tfv,wv->tfw", turned, width_basis, precision=lax.Precision.HIGHEST)
        outputs.append(final.astype(jnp.bfloat16).reshape(FF, BW))
    return jnp.stack(outputs, axis=0)
```

```python
import functools

import jax
import jax.numpy as jnp
from jax import lax
from jax.experimental import pallas as pl
from jax.experimental.pallas import tpu as pltpu
from jax.sharding import PartitionSpec as P

damping_term = 0.1
vmem_limit = 56 * 1024 * 1024


def slot_ranks(block_owner):
    count_blocks = block_owner.shape[0]
    positions = jnp.arange(count_blocks, dtype=jnp.int32)
    earlier = positions[None, :] < positions[:, None]
    same_owner = block_owner[:, None] == block_owner[None, :]
    return jnp.sum(jnp.logical_and(earlier, same_owner).astype(jnp.int32), axis=1)


def largest_tile(extent, limit, unit):
    tile = min(extent, limit)
    while extent % tile or tile % unit:
        tile -= unit
    return tile


def pick_kernel(index_ref, source_ref, out_ref):
    out_ref[...] = source_ref[...]


def pick_blocks(source, index):
    count = index.shape[0]
    block = (1,) + source.shape[1:]
    size = 2 * source.dtype.itemsize * count * source[0].size
    return pl.pallas_call(
        pick_kernel,
        grid_spec=pltpu.PrefetchScalarGridSpec(
            num_scalar_prefetch=1,
            grid=(count,),
            in_specs=[pl.BlockSpec(block, lambda o, index: (index[o], 0, 0))],
            out_specs=pl.BlockSpec(block, lambda o, index: (o, 0, 0)),
        ),
        out_shape=jax.ShapeDtypeStruct((count,) + source.shape[1:], source.dtype),
        cost_estimate=pl.CostEstimate(flops=0, bytes_accessed=size, transcendentals=0),
        name="pick_blocks",
    )(index, source)


def patch_kernel(source_index_ref, block_index_ref, source_ref, whole_ref, out_ref):
    out_ref[...] = source_ref[...]


def patch_blocks(whole, source, source_index, block_index):
    count = source_index.shape[0]
    parts = whole.shape[2] // source.shape[2]
    block = (1,) + source.shape[1:]
    size = 2 * source.dtype.itemsize * source.size
    return pl.pallas_call(
        patch_kernel,
        grid_spec=pltpu.PrefetchScalarGridSpec(
            num_scalar_prefetch=2,
            grid=(count,),
            in_specs=[
                pl.BlockSpec(block, lambda i, source, target: (source[i], 0, 0)),
                pl.BlockSpec(memory_space=pl.ANY),
            ],
            out_specs=pl.BlockSpec(block, lambda i, source, target: (target[i], 0, i % parts)),
        ),
        out_shape=jax.ShapeDtypeStruct(whole.shape, whole.dtype),
        input_output_aliases={3: 0},
        cost_estimate=pl.CostEstimate(flops=0, bytes_accessed=size, transcendentals=0),
        name="patch_blocks",
    )(source_index, block_index, source, whole)


def scaled_kernel(slot, hidden_parts, *refs):
    hidden_refs = refs[:hidden_parts]
    basis_ref, width_ref, width_basis_t_ref, hidden_values_ref, width_values_ref, out_ref, turned_width = refs[hidden_parts:]
    parts, _, columns = width_ref.shape

    @pl.when(pl.program_id(0) == 0)
    def _():
        total = jnp.zeros(turned_width.shape, jnp.float32)
        for part in range(parts):
            total += lax.dot_general(
                width_ref[part],
                width_basis_t_ref[:, part * columns : (part + 1) * columns],
                (((1,), (1,)), ((), ())),
                preferred_element_type=jnp.float32,
            )
        turned_width[...] = total.astype(turned_width.dtype)

    middle = None
    start = 0
    for hidden_ref in hidden_refs:
        turned_hidden = jnp.dot(
            hidden_ref[...], basis_ref[...], preferred_element_type=jnp.float32
        ).astype(jnp.bfloat16)
        stop = start + hidden_ref.shape[0]
        term = lax.dot_general(
            turned_hidden,
            turned_width[start:stop, :],
            (((0,), (0,)), ((), ())),
            preferred_element_type=jnp.float32,
        )
        middle = term if middle is None else middle + term
        start = stop
    tile = basis_ref.shape[1]
    row = hidden_values_ref[0, slot : slot + 1, :].astype(jnp.float32)
    column = jnp.broadcast_to(row, (8, tile)).T[:, :1]
    width_row = width_values_ref[0, slot : slot + 1, :].astype(jnp.float32)
    out_ref[...] = (middle / (column * width_row + damping_term)).astype(out_ref.dtype)


def scaled_block(hidden, basis, slot, width, width_basis_t, hidden_values, width_values):
    tokens = sum(part.shape[0] for part in hidden)
    rows = basis.shape[2]
    features = width_basis_t.shape[0]
    slots = basis.shape[0]
    tile = largest_tile(rows, 512, 128)
    whole = pl.Buffered(1)
    flops = 2 * tokens * rows * (rows + features) + 2 * tokens * features * features
    size = 2 * (tokens * rows + rows * rows + 2 * features * features + rows * features)
    return pl.pallas_call(
        functools.partial(scaled_kernel, slot, len(hidden)),
        grid=(rows // tile,),
        in_specs=[pl.BlockSpec(part.shape, lambda i: (0, 0), pipeline_mode=whole) for part in hidden]
        + [
            pl.BlockSpec((None, rows, tile), lambda i: (slot, 0, i)),
            pl.BlockSpec(width.shape, lambda i: (0, 0, 0), pipeline_mode=whole),
            pl.BlockSpec(width_basis_t.shape, lambda i: (0, 0), pipeline_mode=whole),
            pl.BlockSpec((1, slots, tile), lambda i: (0, 0, i)),
            pl.BlockSpec((1, slots, features), lambda i: (0, 0, 0), pipeline_mode=whole),
        ],
        out_specs=pl.BlockSpec((tile, features), lambda i: (i, 0)),
        out_shape=jax.ShapeDtypeStruct((rows, features), jnp.bfloat16),
        scratch_shapes=[pltpu.VMEM((tokens, features), jnp.bfloat16)],
        compiler_params=pltpu.CompilerParams(vmem_limit_bytes=vmem_limit),
        cost_estimate=pl.CostEstimate(flops=flops, bytes_accessed=size, transcendentals=0),
        name="scaled_block",
    )(*hidden, basis, width, width_basis_t, hidden_values, width_values)


def back_kernel(parts, part_ref, basis_ref, scaled_ref, *refs):
    turned = jnp.dot(
        basis_ref[...], scaled_ref[...], preferred_element_type=jnp.float32
    ).astype(jnp.bfloat16)
    for part in range(parts):
        refs[parts + part][...] = jnp.dot(
            turned, refs[part][...], preferred_element_type=jnp.float32
        ).astype(jnp.bfloat16)


def back_block(basis, slot, scaled, width_basis_t, parts, first_part):
    rows, features = scaled.shape
    tile = largest_tile(rows, 512, 16)
    whole = pl.Buffered(1)
    columns = features // parts
    flops = 2 * rows * features * (rows + features)
    size = 2 * (rows * rows + 2 * rows * features + features * features)

    def column_part(part):
        return lambda i, first: (0, lax.rem(first[0] + part, parts))

    return pl.pallas_call(
        functools.partial(back_kernel, parts),
        grid_spec=pltpu.PrefetchScalarGridSpec(
            num_scalar_prefetch=1,
            grid=(rows // tile,),
            in_specs=[
                pl.BlockSpec((None, tile, rows), lambda i, first: (slot, i, 0)),
                pl.BlockSpec(scaled.shape, lambda i, first: (0, 0), pipeline_mode=whole),
            ]
            + [
                pl.BlockSpec((features, columns), column_part(part), pipeline_mode=whole)
                for part in range(parts)
            ],
            out_specs=[pl.BlockSpec((tile, columns), lambda i, first: (i, 0))] * parts,
        ),
        out_shape=[jax.ShapeDtypeStruct((rows, columns), jnp.bfloat16)] * parts,
        compiler_params=pltpu.CompilerParams(vmem_limit_bytes=vmem_limit),
        cost_estimate=pl.CostEstimate(flops=flops, bytes_accessed=size, transcendentals=0),
        name="back_block",
    )(first_part, basis, scaled, *([width_basis_t] * parts))


def exchange(blocks):
    return lax.all_to_all(blocks, "dp", split_axis=0, concat_axis=0, tiled=True)


def swap_cores(array):
    count = lax.axis_size("dp")
    return lax.ppermute(array, "dp", [(device, device ^ 1) for device in range(count)])


def in_order(first, then):
    return lax.optimization_barrier((first, then))


def where_held(held, count):
    blocks = held.shape[1]
    block_of = jnp.sum(held * jnp.arange(blocks, dtype=jnp.int32), axis=1, dtype=jnp.int32)
    used = jnp.any(held, axis=1)
    some = jnp.argmax(used).astype(jnp.int32)
    holder = jnp.where(used, jnp.arange(count, dtype=jnp.int32), some)
    return block_of, used, holder


def run(
    paired, width_side, hidden_side, block_owner, basis_hidden, basis_width, values_hidden, values_width
):
    dp_count = lax.axis_size("dp")
    tensor_count = lax.axis_size("tensor")
    blocks, local_tokens, rows = hidden_side.shape
    features = width_side.shape[2]
    basis = basis_hidden[0]
    cores = 2
    chips = dp_count // cores
    core = lax.rem(lax.axis_index("dp"), cores)

    ranks = slot_ranks(block_owner)
    owner_ids = jnp.arange(dp_count, dtype=jnp.int32)
    owned = block_owner[None, :] == owner_ids[:, None]
    first_held = jnp.logical_and(owned, (ranks == 0)[None, :])
    second_held = jnp.logical_and(owned, (ranks == 1)[None, :])
    first_block, _, _ = where_held(first_held, dp_count)
    if paired:
        chip_held = jnp.any(second_held.reshape(chips, cores, blocks), axis=1)
        second_block, _, second_holder = where_held(chip_held, chips)
    else:
        second_block, _, second_holder = where_held(second_held, dp_count)
    second_tokens = local_tokens * second_block.shape[0] // dp_count

    columns = features // tensor_count
    width_part = lax.dynamic_slice_in_dim(
        width_side, lax.axis_index("tensor") * columns, columns, 2
    )
    width_out = jnp.concatenate(
        [
            jnp.take(width_part, first_block, axis=0),
            jnp.take(width_part, second_block, axis=0).reshape(dp_count, second_tokens, columns),
        ],
        axis=1,
    )
    width_owned = exchange(width_out)
    width_first = width_owned[:, :local_tokens].reshape(dp_count * local_tokens, columns)
    width_second = width_owned[:, local_tokens:].reshape(dp_count * second_tokens, columns)
    widths = [lax.all_gather(part, "tensor", axis=0) for part in (width_first, width_second)]
    bases_t = [
        lax.all_gather(basis_width[0, slot], "tensor", axis=0, tiled=True).T for slot in range(2)
    ]

    hidden_first = exchange(pick_blocks(hidden_side, first_block))
    hidden_first, hidden_second = in_order(hidden_first, pick_blocks(hidden_side, second_block))
    hidden_second = exchange(hidden_second.reshape(dp_count, second_tokens, rows))

    def scaled_of(slot):
        return scaled_block(
            hiddens[slot], basis, slot, widths[slot], bases_t[slot], values_hidden, values_width
        )

    none = jnp.zeros((1,), jnp.int32)
    hiddens = [[hidden_first.reshape(dp_count * local_tokens, rows)]]
    (result,) = back_block(basis, 0, scaled_of(0), bases_t[0], 1, none)
    hidden_second, result = in_order(hidden_second, result)
    returned = exchange(result.reshape(dp_count, rows // dp_count, features))
    hidden_second = hidden_second.reshape(dp_count * second_tokens, rows)
    hiddens.append([hidden_second])
    if paired:
        hiddens[1].append(swap_cores(hidden_second))
        widths[1] = jnp.concatenate([widths[1], swap_cores(widths[1])], axis=1)
    if paired:
        kept, sent = back_block(
            basis, 1, scaled_of(1), bases_t[1], cores, core.astype(jnp.int32)[None]
        )
        mine = jnp.sum((block_owner == lax.axis_index("dp")).astype(jnp.int32)) == 2
        result = jnp.where(mine, kept, swap_cores(sent))
        source_index = (
            second_holder[:, None] * cores + jnp.arange(cores, dtype=jnp.int32)[None, :]
        ).reshape(-1)
        target_index = jnp.repeat(second_block[second_holder], cores)
    else:
        (result,) = back_block(basis, 1, scaled_of(1), bases_t[1], 1, none)
        source_index = second_holder
        target_index = second_block[second_holder]
    returned_second = exchange(result.reshape(dp_count, rows // dp_count, result.shape[1]))
    return patch_blocks(
        pick_blocks(returned, block_owner), returned_second, source_index, target_index
    )


def body(*arguments):
    block_owner = arguments[2]
    dp_count = lax.axis_size("dp")
    owner_ids = jnp.arange(dp_count, dtype=jnp.int32)
    second = jnp.sum((block_owner[None, :] == owner_ids[:, None]).astype(jnp.int32), axis=1) == 2
    paired = jnp.logical_not(jnp.any(jnp.all(second.reshape(-1, 2), axis=1)))
    return lax.cond(
        paired, functools.partial(run, True), functools.partial(run, False), *arguments
    )


def solution(mesh):
    return jax.shard_map(
        body,
        mesh=mesh,
        in_specs=(
            P(None, "dp", None),
            P(None, "dp", "tensor"),
            P(),
            P("dp", None, "tensor", None),
            P("dp", None, "tensor", None),
            P("dp", None, "tensor"),
            P("dp", None, None),
        ),
        out_specs=P(None, ("tensor", "dp"), None),
        check_vma=False,
    )
```

```python
import functools

import jax
import jax.numpy as jnp
from jax import lax
from jax.experimental import pallas as pl
from jax.experimental.pallas import tpu as pltpu
from jax.sharding import PartitionSpec as P

damping_term = 0.1
vmem_limit = 56 * 1024 * 1024


def slot_ranks(block_owner):
    count_blocks = block_owner.shape[0]
    positions = jnp.arange(count_blocks, dtype=jnp.int32)
    earlier = positions[None, :] < positions[:, None]
    same_owner = block_owner[:, None] == block_owner[None, :]
    return jnp.sum(jnp.logical_and(earlier, same_owner).astype(jnp.int32), axis=1)


def largest_tile(extent, limit, unit):
    tile = min(extent, limit)
    while extent % tile or tile % unit:
        tile -= unit
    return tile


def pick_kernel(index_ref, source_ref, out_ref):
    out_ref[...] = source_ref[...]


def pick_blocks(source, index):
    count = index.shape[0]
    block = (1,) + source.shape[1:]
    size = 2 * source.dtype.itemsize * count * source[0].size
    return pl.pallas_call(
        pick_kernel,
        grid_spec=pltpu.PrefetchScalarGridSpec(
            num_scalar_prefetch=1,
            grid=(count,),
            in_specs=[pl.BlockSpec(block, lambda o, index: (index[o], 0, 0))],
            out_specs=pl.BlockSpec(block, lambda o, index: (o, 0, 0)),
        ),
        out_shape=jax.ShapeDtypeStruct((count,) + source.shape[1:], source.dtype),
        cost_estimate=pl.CostEstimate(flops=0, bytes_accessed=size, transcendentals=0),
        name="pick_blocks",
    )(index, source)


def patch_kernel(source_index_ref, block_index_ref, source_ref, whole_ref, out_ref):
    parts, _, columns = source_ref.shape
    for part in range(parts):
        out_ref[0, :, part * columns : (part + 1) * columns] = source_ref[part]


def patch_blocks(whole, source, source_index, block_index):
    count = source_index.shape[0]
    _, rows, columns = whole.shape
    parts = columns // source.shape[2]
    size = 2 * source.dtype.itemsize * source.size
    return pl.pallas_call(
        patch_kernel,
        grid_spec=pltpu.PrefetchScalarGridSpec(
            num_scalar_prefetch=2,
            grid=(count,),
            in_specs=[
                pl.BlockSpec(
                    (parts,) + source.shape[1:], lambda i, source, target: (source[i], 0, 0)
                ),
                pl.BlockSpec(memory_space=pl.ANY),
            ],
            out_specs=pl.BlockSpec((1, rows, columns), lambda i, source, target: (target[i], 0, 0)),
        ),
        out_shape=jax.ShapeDtypeStruct(whole.shape, whole.dtype),
        input_output_aliases={3: 0},
        cost_estimate=pl.CostEstimate(flops=0, bytes_accessed=size, transcendentals=0),
        name="patch_blocks",
    )(source_index, block_index, source, whole)


def scaled_kernel(slot, count, *refs):
    hidden_refs = refs[:count]
    width_refs = refs[count : 2 * count]
    (
        basis_ref,
        width_basis_t_ref,
        hidden_values_ref,
        width_values_ref,
        out_ref,
        turned_width,
    ) = refs[2 * count :]

    @pl.when(pl.program_id(0) == 0)
    def _():
        start = 0
        for width_ref in width_refs:
            parts, extent, columns = width_ref.shape
            total = jnp.zeros((extent, turned_width.shape[1]), jnp.float32)
            for part in range(parts):
                total += lax.dot_general(
                    width_ref[part],
                    width_basis_t_ref[:, part * columns : (part + 1) * columns],
                    (((1,), (1,)), ((), ())),
                    preferred_element_type=jnp.float32,
                )
            turned_width[start : start + extent, :] = total.astype(turned_width.dtype)
            start += extent

    middle = None
    start = 0
    for hidden_ref in hidden_refs:
        turned_hidden = jnp.dot(
            hidden_ref[...], basis_ref[...], preferred_element_type=jnp.float32
        ).astype(jnp.bfloat16)
        stop = start + hidden_ref.shape[0]
        term = lax.dot_general(
            turned_hidden,
            turned_width[start:stop, :],
            (((0,), (0,)), ((), ())),
            preferred_element_type=jnp.float32,
        )
        middle = term if middle is None else middle + term
        start = stop
    tile = basis_ref.shape[1]
    row = hidden_values_ref[0, slot : slot + 1, :].astype(jnp.float32)
    column = jnp.broadcast_to(row, (8, tile)).T[:, :1]
    width_row = width_values_ref[0, slot : slot + 1, :].astype(jnp.float32)
    out_ref[...] = (middle / (column * width_row + damping_term)).astype(out_ref.dtype)


def scaled_block(hidden, basis, slot, width, width_basis_t, hidden_values, width_values):
    tokens = sum(part.shape[0] for part in hidden)
    rows = basis.shape[2]
    features = width_basis_t.shape[0]
    slots = basis.shape[0]
    tile = largest_tile(rows, 1024, 128)
    whole = pl.Buffered(1)
    flops = 2 * tokens * rows * (rows + features) + 2 * tokens * features * features
    size = 2 * (tokens * rows + rows * rows + 2 * features * features + rows * features)
    return pl.pallas_call(
        functools.partial(scaled_kernel, slot, len(hidden)),
        grid=(rows // tile,),
        in_specs=[pl.BlockSpec(part.shape, lambda i: (0, 0), pipeline_mode=whole) for part in hidden]
        + [pl.BlockSpec(part.shape, lambda i: (0, 0, 0), pipeline_mode=whole) for part in width]
        + [
            pl.BlockSpec((None, rows, tile), lambda i: (slot, 0, i)),
            pl.BlockSpec(width_basis_t.shape, lambda i: (0, 0), pipeline_mode=whole),
            pl.BlockSpec((1, slots, tile), lambda i: (0, 0, i)),
            pl.BlockSpec((1, slots, features), lambda i: (0, 0, 0), pipeline_mode=whole),
        ],
        out_specs=pl.BlockSpec((tile, features), lambda i: (i, 0)),
        out_shape=jax.ShapeDtypeStruct((rows, features), jnp.bfloat16),
        scratch_shapes=[pltpu.VMEM((tokens, features), jnp.bfloat16)],
        compiler_params=pltpu.CompilerParams(vmem_limit_bytes=vmem_limit),
        cost_estimate=pl.CostEstimate(flops=flops, bytes_accessed=size, transcendentals=0),
        name="scaled_block",
    )(*hidden, *width, basis, width_basis_t, hidden_values, width_values)


def back_kernel(parts, part_ref, basis_ref, scaled_ref, *refs):
    turned = jnp.dot(
        basis_ref[...], scaled_ref[...], preferred_element_type=jnp.float32
    ).astype(jnp.bfloat16)
    for part in range(parts):
        refs[parts + part][...] = jnp.dot(
            turned, refs[part][...], preferred_element_type=jnp.float32
        ).astype(jnp.bfloat16)


def back_block(basis, slot, scaled, width_basis_t, parts, first_part):
    rows, features = scaled.shape
    tile = largest_tile(rows, 1024, 16)
    whole = pl.Buffered(1)
    columns = features // parts
    flops = 2 * rows * features * (rows + features)
    size = 2 * (rows * rows + 2 * rows * features + features * features)

    def column_part(part):
        return lambda i, first: (0, lax.rem(first[0] + part, parts))

    return pl.pallas_call(
        functools.partial(back_kernel, parts),
        grid_spec=pltpu.PrefetchScalarGridSpec(
            num_scalar_prefetch=1,
            grid=(rows // tile,),
            in_specs=[
                pl.BlockSpec((None, tile, rows), lambda i, first: (slot, i, 0)),
                pl.BlockSpec(scaled.shape, lambda i, first: (0, 0), pipeline_mode=whole),
            ]
            + [
                pl.BlockSpec((features, columns), column_part(part), pipeline_mode=whole)
                for part in range(parts)
            ],
            out_specs=[pl.BlockSpec((tile, columns), lambda i, first: (i, 0))] * parts,
        ),
        out_shape=[jax.ShapeDtypeStruct((rows, columns), jnp.bfloat16)] * parts,
        compiler_params=pltpu.CompilerParams(vmem_limit_bytes=vmem_limit),
        cost_estimate=pl.CostEstimate(flops=flops, bytes_accessed=size, transcendentals=0),
        name="back_block",
    )(first_part, basis, scaled, *([width_basis_t] * parts))


def exchange(blocks):
    return lax.all_to_all(blocks, "dp", split_axis=0, concat_axis=0, tiled=True)


def swap_cores(array):
    count = lax.axis_size("dp")
    return lax.ppermute(array, "dp", [(device, device ^ 1) for device in range(count)])


def in_order(first, then):
    return lax.optimization_barrier((first, then))


def where_held(held, count):
    blocks = held.shape[1]
    block_of = jnp.sum(held * jnp.arange(blocks, dtype=jnp.int32), axis=1, dtype=jnp.int32)
    used = jnp.any(held, axis=1)
    some = jnp.argmax(used).astype(jnp.int32)
    holder = jnp.where(used, jnp.arange(count, dtype=jnp.int32), some)
    return block_of, used, holder


def run(
    paired, width_side, hidden_side, block_owner, basis_hidden, basis_width, values_hidden, values_width
):
    dp_count = lax.axis_size("dp")
    tensor_count = lax.axis_size("tensor")
    blocks, local_tokens, rows = hidden_side.shape
    features = width_side.shape[2]
    basis = basis_hidden[0]
    cores = 2
    chips = dp_count // cores
    core = lax.rem(lax.axis_index("dp"), cores)

    ranks = slot_ranks(block_owner)
    owner_ids = jnp.arange(dp_count, dtype=jnp.int32)
    owned = block_owner[None, :] == owner_ids[:, None]
    first_held = jnp.logical_and(owned, (ranks == 0)[None, :])
    second_held = jnp.logical_and(owned, (ranks == 1)[None, :])
    first_block, _, _ = where_held(first_held, dp_count)
    if paired:
        chip_held = jnp.any(second_held.reshape(chips, cores, blocks), axis=1)
        second_block, _, second_holder = where_held(chip_held, chips)
    else:
        second_block, _, second_holder = where_held(second_held, dp_count)
    second_tokens = local_tokens * second_block.shape[0] // dp_count

    columns = features // tensor_count
    width_part = lax.dynamic_slice_in_dim(
        width_side, lax.axis_index("tensor") * columns, columns, 2
    )
    width_out = jnp.concatenate(
        [
            jnp.take(width_part, first_block, axis=0),
            jnp.take(width_part, second_block, axis=0).reshape(dp_count, second_tokens, columns),
        ],
        axis=1,
    )
    width_owned = exchange(width_out)
    width_first = width_owned[:, :local_tokens].reshape(dp_count * local_tokens, columns)
    width_second = width_owned[:, local_tokens:].reshape(dp_count * second_tokens, columns)
    widths = [[lax.all_gather(part, "tensor", axis=0)] for part in (width_first, width_second)]
    bases_t = [
        lax.all_gather(basis_width[0, slot], "tensor", axis=0, tiled=True).T for slot in range(2)
    ]

    hidden_first = exchange(pick_blocks(hidden_side, first_block))
    hidden_first, hidden_second = in_order(hidden_first, pick_blocks(hidden_side, second_block))
    hidden_second = exchange(hidden_second.reshape(dp_count, second_tokens, rows))

    def scaled_of(slot):
        return scaled_block(
            hiddens[slot], basis, slot, widths[slot], bases_t[slot], values_hidden, values_width
        )

    none = jnp.zeros((1,), jnp.int32)
    hiddens = [[hidden_first.reshape(dp_count * local_tokens, rows)]]
    scaled = scaled_of(0)
    hidden_second = hidden_second.reshape(dp_count * second_tokens, rows)
    (hidden_second, widths[1]), scaled = in_order((hidden_second, widths[1]), scaled)
    hiddens.append([hidden_second])
    if paired:
        hiddens[1].append(swap_cores(hidden_second))
        widths[1] = [widths[1][0], swap_cores(widths[1][0])]
    (result,) = back_block(basis, 0, scaled, bases_t[0], 1, none)
    (hiddens[1], widths[1]), result = in_order((hiddens[1], widths[1]), result)
    returned = exchange(result.reshape(dp_count, rows // dp_count, features))
    target_index = second_block[second_holder]
    if paired:
        kept, sent = back_block(
            basis, 1, scaled_of(1), bases_t[1], cores, core.astype(jnp.int32)[None]
        )
        mine = jnp.sum((block_owner == lax.axis_index("dp")).astype(jnp.int32)) == 2
        result = jnp.where(mine, kept, swap_cores(sent))
    else:
        (result,) = back_block(basis, 1, scaled_of(1), bases_t[1], 1, none)
    returned_second = exchange(result.reshape(dp_count, rows // dp_count, result.shape[1]))
    return patch_blocks(
        pick_blocks(returned, block_owner), returned_second, second_holder, target_index
    )


def body(*arguments):
    block_owner = arguments[2]
    dp_count = lax.axis_size("dp")
    owner_ids = jnp.arange(dp_count, dtype=jnp.int32)
    second = jnp.sum((block_owner[None, :] == owner_ids[:, None]).astype(jnp.int32), axis=1) == 2
    paired = jnp.logical_not(jnp.any(jnp.all(second.reshape(-1, 2), axis=1)))
    return lax.cond(
        paired, functools.partial(run, True), functools.partial(run, False), *arguments
    )


def solution(mesh):
    return jax.shard_map(
        body,
        mesh=mesh,
        in_specs=(
            P(None, "dp", None),
            P(None, "dp", "tensor"),
            P(),
            P("dp", None, "tensor", None),
            P("dp", None, "tensor", None),
            P("dp", None, "tensor"),
            P("dp", None, None),
        ),
        out_specs=P(None, ("tensor", "dp"), None),
        check_vma=False,
    )
```
